256 devices in a mesh: ctx: 64 (over z, y, x_lo), head: 4 (over x_hi, core).
Axes of the slice: x: 4 (x_hi: 2, x_lo: 2; x = x_hi * 2 + x_lo), y: 4, z: 8, core: 2. Of those that a mesh axis runs over, the one named last changes fastest.
Arguments:
- queries: bfloat16 [8192, 2048], P('ctx', 'head'), may hold values from -4.5 to 4.5
- key_vectors: bfloat16 [8192, 2048], P('ctx', 'head'), may hold values from -4.5 to 4.5
- value_vectors: bfloat16 [8192, 2048], P('ctx', 'head'), may hold values from -6 to 6
- out_weight: bfloat16 [2048, 4096], P('head'), may hold values from -0.125 to 0.125
Outputs:
- layer_out: float32 [8192, 4096], P(('ctx', 'head'))
The draws below stay inside these ranges and needn't reach their ends.
All inputs are finite; a program needn't handle non-finite values.
Results may differ from the reference program's by a relative error of at most 0.009.
Values may be sent and summed in bfloat16 or wider, within the bound.
No kernel may reach another device: no remote copies, remote signals or barrier semaphores. Data moves between devices by JAX's collectives and lax.ppermute only.
A program may use at most 128 MiB of HBM per device.

```python
import math
import jax
import jax.numpy as jnp
from jax import lax

D = 4096
DH = 128
HEADS = 16
SEQ = 8192


def draw_queries(key, part):
    key = jax.random.fold_in(key, 1)
    entries = jnp.clip(1.7 * jax.random.normal(key, (SEQ, HEADS, DH), jnp.float32), -4.5, 4.5)
    return entries.reshape(SEQ, HEADS * DH).astype(jnp.bfloat16)


def draw_key_vectors(key, part):
    key = jax.random.fold_in(key, 2)
    entries = jnp.clip(1.7 * jax.random.normal(key, (SEQ, HEADS, DH), jnp.float32), -4.5, 4.5)
    return entries.reshape(SEQ, HEADS * DH).astype(jnp.bfloat16)


def steps_of(rng, shape, split, least, high):
    gain, own = 1.0, jax.random.fold_in(rng, 6)
    for axis_at, parts in split:
        draws = jnp.exp(jax.random.uniform(jax.random.fold_in(own, axis_at), (parts,), jnp.float32, least / len(split), high / len(split)))
        gain = gain * jnp.repeat(draws, shape[axis_at] // parts).reshape([-1 if axis == axis_at else 1 for axis in range(len(shape))])
    return gain


def centred(stream_key, dims, deviation, limit, cuts=(), held_as=jnp.bfloat16):
    values = jax.random.normal(stream_key, dims, jnp.float32) * deviation
    if len(cuts) > 0:
        values = steps_of(stream_key, dims, cuts, -0.22, 0.18) * values
    return jnp.clip(values, min=-limit, max=limit).astype(held_as)


def setup_inputs(seed: int = 0) -> dict:
    key_of = jax.random.split(jax.random.key(seed), 5)
    queries = draw_queries(jax.random.fold_in(key_of[4], 71), 0)
    key_vectors = draw_key_vectors(jax.random.fold_in(key_of[4], 71), 0)
    value_vectors = centred(key_of[2], (SEQ, HEADS * DH), 1.0, 6.0, ((0, 64), (1, 4)))
    out_weight = centred(key_of[3], (HEADS * DH, D), (HEADS * DH) ** -0.5, 0.125, ((0, 4),))
    return {"queries": queries, "key_vectors": key_vectors, "value_vectors": value_vectors, "out_weight": out_weight}


def head_attention(head_inputs):
    head_queries, head_keys, head_values = head_inputs
    block_rows = math.gcd(SEQ, 1024)
    score_scale = DH ** -0.5

    def attend_rows(query_block):
        scores = jnp.dot(query_block, head_keys.T, preferred_element_type=jnp.float32) * score_scale
        row_peak = jnp.max(scores, axis=1, keepdims=True)
        exponent = jnp.exp(scores - row_peak)
        row_sum = jnp.sum(exponent, axis=1, keepdims=True)
        summed = jnp.dot(exponent.astype(jnp.bfloat16), head_values, preferred_element_type=jnp.float32)
        return (summed / row_sum).astype(jnp.bfloat16)

    blocks = head_queries.reshape(SEQ // block_rows, block_rows, DH)
    return lax.map(attend_rows, blocks).reshape(SEQ, DH)


def reference(queries, key_vectors, value_vectors, out_weight):
    def split_heads(matrix):
        return matrix.reshape(SEQ, HEADS, DH).transpose(1, 0, 2)

    attended = lax.map(head_attention, (split_heads(queries), split_heads(key_vectors), split_heads(value_vectors)))
    attended = attended.transpose(1, 0, 2).reshape(SEQ, HEADS * DH)
    return jnp.dot(attended, out_weight, preferred_element_type=jnp.float32)
```

```python
import functools

import jax
import jax.numpy as jnp
from jax import lax
from jax.experimental import pallas as pl
from jax.experimental.pallas import tpu as pltpu
from jax.sharding import Mesh, PartitionSpec as P

DH = 128
AXES = {"z": 8, "y": 4, "xl": 2, "xh": 2, "c": 2}
PLANE = ("y", "xl")
SLOTS = [(dy, f) for dy in range(4) for f in range(2)]
LOG2E = 1.4426950408889634
TOK = 128
HEADS_LOCAL = 4
STAT_ROWS = 16
VMEM = 48 * 1024 * 1024


def ring(x, by):
    return lax.ppermute(x, "z", [(i, (i + by) % AXES["z"]) for i in range(AXES["z"])])


def plane_perm(dy, f, back):
    pairs = []
    for y in range(4):
        for xl in range(2):
            src, dst = y * 2 + xl, ((y + dy) % 4) * 2 + (xl ^ f)
            pairs.append((dst, src) if back else (src, dst))
    return pairs


def flip(x, axis):
    return lax.ppermute(x, axis, [(0, 1), (1, 0)])


def dot(a, b, dims):
    return lax.dot_general(a, b, (dims, ((), ())), preferred_element_type=jnp.float32)


def attend_kernel(n_blocks, first, last, *refs):
    refs = list(refs)
    take = lambda n: [refs.pop(0) for _ in range(n)]
    q_refs, k_refs, v_refs = take(8), take(n_blocks), take(n_blocks)
    if not first:
        o_in, ml_in = take(2)
    if last:
        out_refs = take(8)
        (stat,) = take(1)
    else:
        o_out, ml_out = take(2)
    head = pl.program_id(0)
    scale = LOG2E * DH**-0.5
    keys = jnp.concatenate([r[...] for r in k_refs], axis=0)
    values = jnp.concatenate([r[...] for r in v_refs], axis=0)
    for j in range(4):
        cols = pl.ds(j * 256, 256)
        queries = jnp.concatenate([q_refs[2 * j][...], q_refs[2 * j + 1][...]], axis=0)
        s = dot(keys, queries, ((1,), (1,)))
        peak = jnp.max(s, axis=0, keepdims=True)
        if not first:
            old_peak = ml_in[0, 0:1, cols]
            peak = jnp.maximum(peak, old_peak)
        p = jnp.exp2((s - peak) * scale)
        total = jnp.sum(p, axis=0, keepdims=True)
        summed = dot(values, p.astype(jnp.bfloat16), ((0,), (0,)))
        if not first:
            decay = jnp.exp2((old_peak - peak) * scale)
            total = total + ml_in[0, 1:2, cols] * decay
            summed = summed + o_in[:, cols] * decay
        if last:
            summed = (summed / total).astype(jnp.bfloat16)
            for i in range(2):
                rows = pl.ds(pl.multiple_of(head * DH, DH), DH)
                out_refs[2 * j + i][rows, :] = summed[:, i * 128 : (i + 1) * 128]
            stat[head, :, cols] = peak * scale + jnp.log2(total)
        else:
            o_out[:, cols] = summed
            ml_out[0, 0:1, cols] = peak
            ml_out[0, 1:2, cols] = total
    if last:

        @pl.when(head == HEADS_LOCAL - 1)
        def _():
            lse = jnp.concatenate([stat[h] for h in range(HEADS_LOCAL)], axis=0)
            hi = lse.astype(jnp.bfloat16).astype(jnp.float32)
            mid = (lse - hi).astype(jnp.bfloat16).astype(jnp.float32)
            low = lse - hi - mid
            rows = jnp.concatenate([hi, mid, low, jnp.zeros_like(hi)], axis=0).astype(jnp.bfloat16)
            for r in range(8):
                out_refs[r][pl.ds(HEADS_LOCAL * DH, STAT_ROWS), :] = rows[:, r * 128 : (r + 1) * 128]


def attend(q_slots, keys, values, state, last):
    n = len(keys)
    first = state is None
    block = pl.BlockSpec((TOK, DH), lambda h: (0, h))
    o_spec = pl.BlockSpec((DH, 8 * TOK), lambda h: (h, 0))
    ml_spec = pl.BlockSpec((1, 2, 8 * TOK), lambda h: (h, 0, 0))
    in_specs = [block] * (8 + 2 * n) + ([] if first else [o_spec, ml_spec])
    if last:
        rows = HEADS_LOCAL * DH + STAT_ROWS
        out_shape = [jax.ShapeDtypeStruct((rows, TOK), jnp.bfloat16)] * 8
        out_specs = [pl.BlockSpec((rows, TOK), lambda h: (0, 0))] * 8
        scratch = [pltpu.VMEM((HEADS_LOCAL, 1, 8 * TOK), jnp.float32)]
    else:
        out_shape = [
            jax.ShapeDtypeStruct((HEADS_LOCAL * DH, 8 * TOK), jnp.float32),
            jax.ShapeDtypeStruct((HEADS_LOCAL, 2, 8 * TOK), jnp.float32),
        ]
        out_specs = [o_spec, ml_spec]
        scratch = []
    elements = HEADS_LOCAL * 8 * TOK * n * TOK
    return pl.pallas_call(
        functools.partial(attend_kernel, n, first, last),
        grid=(HEADS_LOCAL,),
        in_specs=in_specs,
        out_specs=out_specs,
        out_shape=out_shape,
        scratch_shapes=scratch,
        compiler_params=pltpu.CompilerParams(vmem_limit_bytes=VMEM),
        cost_estimate=pl.CostEstimate(
            flops=elements * DH * 4, transcendentals=elements, bytes_accessed=4 << 20
        ),
        name="attend",
    )(*q_slots, *keys, *values, *(() if first else state))


def project_kernel(place, *refs):
    parts, w_ref, send, keep, att = refs[:8], refs[8], refs[9], refs[10], refs[11]

    @pl.when(pl.program_id(0) == 0)
    def _():
        lse = []
        for r in range(8):
            s = parts[r][pl.ds(HEADS_LOCAL * DH, STAT_ROWS), :].astype(jnp.float32)
            lse.append(s[0:4] + s[4:8] + s[8:12])
        top = functools.reduce(jnp.maximum, lse)
        weights = [jnp.exp2(x - top) for x in lse]
        inverse = 1.0 / sum(weights)
        weights = [w * inverse for w in weights]
        c, xh = place[0], place[1]
        for h in range(HEADS_LOCAL):
            rows = pl.ds(h * DH, DH)
            merged = sum(parts[r][rows, :].astype(jnp.float32) * weights[r][h : h + 1, :] for r in range(8))
            tokens = merged.T.astype(jnp.bfloat16)
            for to_xh in range(2):
                for to_c in range(2):
                    here = (to_c ^ 1) * 2 + to_xh
                    there = jnp.where(c == to_c, 2, 0) + jnp.where(xh == to_xh, 1, 0)
                    piece = tokens[(to_xh * 2 + to_c) * 32 : (to_xh * 2 + to_c) * 32 + 32]
                    del here
                    att[pl.ds(pl.multiple_of(there * 32, 32), 32), pl.ds(h * DH, DH)] = piece

    product = dot(att[...], w_ref[...], ((1,), (0,)))
    send[...] = product[:64].astype(jnp.bfloat16)
    keep[...] = product[64:]


def project(place, parts, weight):
    rows = HEADS_LOCAL * DH + STAT_ROWS
    width = weight.shape[1]
    tile = 1024
    return pl.pallas_call(
        project_kernel,
        grid_spec=pltpu.PrefetchScalarGridSpec(
            num_scalar_prefetch=1,
            grid=(width // tile,),
            in_specs=[pl.BlockSpec((rows, TOK), lambda i, p: (0, 0))] * 8
            + [pl.BlockSpec((HEADS_LOCAL * DH, tile), lambda i, p: (0, i))],
            out_specs=[pl.BlockSpec((64, tile), lambda i, p: (0, i))] * 2,
            scratch_shapes=[pltpu.VMEM((TOK, HEADS_LOCAL * DH), jnp.bfloat16)],
        ),
        out_shape=[
            jax.ShapeDtypeStruct((64, width), jnp.bfloat16),
            jax.ShapeDtypeStruct((64, width), jnp.float32),
        ],
        compiler_params=pltpu.CompilerParams(vmem_limit_bytes=VMEM),
        cost_estimate=pl.CostEstimate(
            flops=2 * TOK * HEADS_LOCAL * DH * width, transcendentals=4096, bytes_accessed=6 << 20
        ),
        name="merge_project",
    )(place, *parts, weight)


def body(queries, key_vectors, value_vectors, out_weight):
    up = (key_vectors, value_vectors)
    down = up
    up_blocks, down_blocks = [], []
    for step in range(3):
        up = tuple(ring(x, 1) for x in up)
        down = tuple(ring(x, -1) for x in down)
        up_blocks.append(up)
        down_blocks.append(down)
        if step == 0:
            q_slots = [
                queries if slot == (0, 0) else lax.ppermute(queries, PLANE, plane_perm(*slot, False))
                for slot in SLOTS
            ]
    far = (ring(up[0], 1), ring(down[1], -1))
    near = [(key_vectors, value_vectors)] + up_blocks[:2] + down_blocks[:2]
    state = attend(q_slots, [b[0] for b in near], [b[1] for b in near], None, False)
    third = [up_blocks[2], down_blocks[2]]
    state = attend(q_slots, [b[0] for b in third], [b[1] for b in third], state, False)
    parts = attend(q_slots, [far[0]], [far[1]], state, True)
    parts = [
        part if slot == (0, 0) else lax.ppermute(part, PLANE, plane_perm(*slot, True))
        for slot, part in zip(SLOTS, parts)
    ]
    place = jnp.stack([lax.axis_index("c"), lax.axis_index("xh")]).astype(jnp.int32)
    send, keep = project(place, parts, out_weight)
    both = keep + flip(send, "c").astype(jnp.float32)
    return both[32:] + flip(both[:32].astype(jnp.bfloat16), "xh").astype(jnp.float32)


def solution(mesh):
    fine = Mesh(mesh.devices.reshape(tuple(AXES.values())), tuple(AXES))
    ctx, head = ("z", "y", "xl"), ("xh", "c")
    placed = (P(ctx, head), P(ctx, head), P(ctx, head), P(head, None))
    return jax.shard_map(
        body, mesh=fine, in_specs=placed, out_specs=P(ctx + head, None), check_vma=False
    )
```

```python
import functools

import jax
import jax.numpy as jnp
from jax import lax
from jax.experimental import pallas as pl
from jax.experimental.pallas import tpu as pltpu
from jax.sharding import Mesh, PartitionSpec as P

DH = 128
AXES = {"z": 8, "y": 4, "xl": 2, "xh": 2, "c": 2}
PLANE = ("y", "xl")
SLOTS = ((0, 0), (0, 1), (2, 0), (2, 1), (-1, 0), (-1, 1), (1, 0), (1, 1))
FIRST_OUT = (2, 3, 5, 7, 4, 6, 1)
SPAN = 4
LOG2E = 1.4426950408889634
TOK = 128
HEADS_LOCAL = 4
STAT_ROWS = 16
VMEM = 24 * 1024 * 1024
CHUNK = 1024


def shift(x, axis, by):
    n = AXES[axis]
    return lax.ppermute(x, axis, [(i, (i + by) % n) for i in range(n)])


def to_slot(x, slot):
    dy, f = slot
    pairs = [(y * 2 + xl, (y + dy) % 4 * 2 + (xl ^ f)) for y in range(4) for xl in range(2)]
    return lax.ppermute(x, PLANE, pairs)


def flip(x, axis):
    return lax.ppermute(x, axis, [(0, 1), (1, 0)])


def dot(a, b, dims):
    return lax.dot_general(a, b, (dims, ((), ())), preferred_element_type=jnp.float32)


def pack_kernel(k, v, own):
    own[:TOK] = k[...]
    own[TOK:] = v[...]


def pack(keys, values):
    return pl.pallas_call(
        pack_kernel,
        grid=(1,),
        in_specs=[pl.BlockSpec(keys.shape, lambda i: (0, 0))] * 2,
        out_specs=pl.BlockSpec((2 * TOK, keys.shape[1]), lambda i: (0, 0)),
        out_shape=jax.ShapeDtypeStruct((2 * TOK, keys.shape[1]), jnp.bfloat16),
        name="pack",
    )(keys, values)


def attend_kernel(n_blocks, last, *refs):
    refs = list(refs)
    take = lambda n: [refs.pop(0) for _ in range(n)]
    q_refs, kv_refs = take(5), take(n_blocks)
    if last:
        far_k, far_v, o_in, ml_in = take(4)
        out_refs = take(8)
    else:
        o_out, ml_out = take(2)
    scale = LOG2E * DH**-0.5

    def operands(h):
        lanes = slice(h * DH, (h + 1) * DH)
        keys = [r[:TOK, lanes] for r in kv_refs]
        values = [r[TOK:, lanes] for r in kv_refs]
        if last:
            keys.append(far_k[:, lanes])
            values.append(far_v[:, lanes])
        return lanes, jnp.concatenate(keys, axis=0), jnp.concatenate(values, axis=0).T

    def scores(lanes, keys, j):
        pieces = q_refs[:3] if j == 0 else q_refs[3:]
        return dot(keys, jnp.concatenate([r[:, lanes] for r in pieces], axis=0), ((1,), (1,)))

    work = []
    for h in range(HEADS_LOCAL):
        lanes, keys, values = operands(h)
        for j in range(8 // SPAN):
            work.append((h, j, lanes, keys, values))
    lse = [[None] * (8 // SPAN) for _ in range(HEADS_LOCAL)]
    ahead = scores(*work[0][2:4], work[0][1])
    for i, (h, j, _, _, values) in enumerate(work):
        s = ahead
        if i + 1 < len(work):
            ahead = scores(*work[i + 1][2:4], work[i + 1][1])
        cols = slice(j * SPAN * TOK, (j + 1) * SPAN * TOK)
        rows = slice(h * DH, (h + 1) * DH)
        peak = jnp.max(s, axis=0, keepdims=True)
        if last:
            old_peak = ml_in[h, 0:1, cols]
            peak = jnp.maximum(peak, old_peak)
        p = jnp.exp2((s - peak) * scale)
        total = jnp.sum(p, axis=0, keepdims=True)
        summed = dot(values, p.astype(jnp.bfloat16), ((1,), (0,)))
        if last:
            decay = jnp.exp2((old_peak - peak) * scale)
            total = total + ml_in[h, 1:2, cols] * decay
            inverse = 1.0 / total
            summed = (summed * inverse + o_in[rows, cols] * (decay * inverse)).astype(jnp.bfloat16)
            for i in range(SPAN):
                out_refs[j * SPAN + i][rows, :] = summed[:, i * TOK : (i + 1) * TOK]
            lse[h][j] = peak * scale + jnp.log2(total)
        else:
            o_out[rows, cols] = summed
            ml_out[h, 0:1, cols] = peak
            ml_out[h, 1:2, cols] = total
    if last:
        whole = jnp.concatenate([jnp.concatenate(x, axis=1) for x in lse], axis=0)
        hi = whole.astype(jnp.bfloat16).astype(jnp.float32)
        mid = (whole - hi).astype(jnp.bfloat16).astype(jnp.float32)
        low = whole - hi - mid
        stats = jnp.concatenate([hi, mid, low, jnp.zeros_like(hi)], axis=0).astype(jnp.bfloat16)
        for r in range(8):
            out_refs[r][HEADS_LOCAL * DH :, :] = stats[:, r * TOK : (r + 1) * TOK]


def attend(queries, blocks, far, state):
    last = far is not None
    whole = lambda x: pl.BlockSpec(x.shape, lambda i: (0,) * len(x.shape))
    operands = [*queries, *blocks] + ([*far, *state] if last else [])
    if last:
        out_shape = [
            jax.ShapeDtypeStruct((HEADS_LOCAL * DH + STAT_ROWS, TOK), jnp.bfloat16)
        ] * 8
    else:
        out_shape = [
            jax.ShapeDtypeStruct((HEADS_LOCAL * DH, 8 * TOK), jnp.float32),
            jax.ShapeDtypeStruct((HEADS_LOCAL, 2, 8 * TOK), jnp.float32),
        ]
    elements = HEADS_LOCAL * 8 * TOK * (len(blocks) + last) * TOK
    return pl.pallas_call(
        functools.partial(attend_kernel, len(blocks), last),
        grid=(1,),
        in_specs=[whole(x) for x in operands],
        out_specs=[whole(x) for x in out_shape],
        out_shape=out_shape,
        compiler_params=pltpu.CompilerParams(vmem_limit_bytes=VMEM),
        cost_estimate=pl.CostEstimate(
            flops=elements * DH * 12, transcendentals=elements, bytes_accessed=4 << 20
        ),
        name="attend",
    )(*operands)


def merge_kernel(place, *refs):
    parts, w_ref, sends, keeps = refs[:8], refs[8], refs[9:11], refs[11:13]
    att = refs[13]
    lse = []
    for r in range(8):
        s = parts[r][HEADS_LOCAL * DH :, :].astype(jnp.float32)
        lse.append(s[0:4] + s[4:8] + s[8:12])
    top = functools.reduce(jnp.maximum, lse)
    weights = [jnp.exp2(x - top) for x in lse]
    inverse = 1.0 / sum(weights)
    weights = [w * inverse for w in weights]
    c, xh = place[0], place[1]
    for h in range(HEADS_LOCAL):
        rows = slice(h * DH, (h + 1) * DH)
        merged = sum(parts[r][rows, :].astype(jnp.float32) * weights[r][h : h + 1, :] for r in range(8))
        tokens = merged.T.astype(jnp.bfloat16)
        for to in range(4):
            there = jnp.where(xh == to // 2, 2, 0) + jnp.where(c == to % 2, 1, 0)
            att[pl.ds(pl.multiple_of(there * 32, 32), 32), rows] = tokens[to * 32 : to * 32 + 32]
    for at in range(0, w_ref.shape[1], CHUNK):
        cols = slice(at, at + CHUNK)
        product = dot(att[...], w_ref[:, cols], ((1,), (0,)))
        for side in range(2):
            sends[side][:, cols] = product[side * 64 : side * 64 + 32].astype(jnp.bfloat16)
            keeps[side][:, cols] = product[side * 64 + 32 : side * 64 + 64]


def project(place, parts, weight):
    depth, width = weight.shape
    whole = lambda x: pl.BlockSpec(x.shape, lambda i, p: (0,) * len(x.shape))
    out_shape = [
        jax.ShapeDtypeStruct((32, width), dtype)
        for dtype in (jnp.bfloat16, jnp.bfloat16, jnp.float32, jnp.float32)
    ]
    return pl.pallas_call(
        merge_kernel,
        grid_spec=pltpu.PrefetchScalarGridSpec(
            num_scalar_prefetch=1,
            grid=(1,),
            in_specs=[whole(x) for x in parts] + [pl.BlockSpec(memory_space=pltpu.VMEM)],
            out_specs=[whole(x) for x in out_shape],
            scratch_shapes=[pltpu.VMEM((TOK, depth), jnp.bfloat16)],
        ),
        out_shape=out_shape,
        compiler_params=pltpu.CompilerParams(vmem_limit_bytes=VMEM),
        cost_estimate=pl.CostEstimate(
            flops=2 * TOK * depth * width, transcendentals=4096, bytes_accessed=6 << 20
        ),
        name="merge_project",
    )(place, *parts, weight)


def body(queries, key_vectors, value_vectors, out_weight):
    own = pack(key_vectors, value_vectors)
    pair = pack(queries, flip(queries, "xl"))
    up, down = shift(own, "z", 1), shift(own, "z", -1)
    blocks = [own, up, down]
    up, down, pair = lax.optimization_barrier((up, down, pair))
    above, below = shift(pair, "y", 1), shift(pair, "y", -1)
    up, down = shift(up, "z", 1), shift(down, "z", -1)
    blocks += [up, down]
    up, down, above, below = lax.optimization_barrier((up, down, above, below))
    up, down = shift(up, "z", 1), shift(down, "z", -1)
    blocks += [up, down]
    far = (shift(up[:TOK], "z", 1), shift(down[TOK:], "z", -1))
    q_parts = [pair, shift(above[:TOK], "y", 1), shift(below[TOK:], "y", -1), above, below]
    state = attend(q_parts, blocks, None, None)
    parts = attend(q_parts, [], far, state)
    parts = list(parts)
    for r in FIRST_OUT:
        parts[r] = to_slot(parts[r], SLOTS[r])
    place = jnp.stack([lax.axis_index("c"), lax.axis_index("xh")]).astype(jnp.int32)
    send_other, send_own, keep_other, keep_own = project(place, parts, out_weight)
    other = keep_other + flip(send_other, "c").astype(jnp.float32)
    arrived = flip(other.astype(jnp.bfloat16), "xh").astype(jnp.float32)
    return keep_own + flip(send_own, "c").astype(jnp.float32) + arrived


def solution(mesh):
    fine = Mesh(mesh.devices.reshape(tuple(AXES.values())), tuple(AXES))
    ctx, head = ("z", "y", "xl"), ("xh", "c")
    placed = (P(ctx, head), P(ctx, head), P(ctx, head), P(head, None))
    return jax.shard_map(
        body, mesh=fine, in_specs=placed, out_specs=P(ctx + head, None), check_vma=False
    )
```

```python
import functools

import jax
import jax.numpy as jnp
from jax import lax
from jax.experimental import pallas as pl
from jax.experimental.pallas import tpu as pltpu
from jax.sharding import Mesh, PartitionSpec as P

DH = 128
AXES = {"z": 8, "y": 4, "xl": 2, "xh": 2, "c": 2}
PLANE = ("y", "xl")
SLOTS = ((0, 0), (0, 1), (2, 0), (2, 1), (-1, 0), (-1, 1), (1, 0), (1, 1))
FIRST_OUT = (2, 3, 5, 7, 4, 6, 1)
SPAN = 4
LOG2E = 1.4426950408889634
TOK = 128
HEADS_LOCAL = 4
STAT_ROWS = 16
VMEM = 13 * 1024 * 1024
CHUNK = 1024


def shift(x, axis, by):
    n = AXES[axis]
    return lax.ppermute(x, axis, [(i, (i + by) % n) for i in range(n)])


def to_slot(x, slot):
    dy, f = slot
    pairs = [(y * 2 + xl, (y + dy) % 4 * 2 + (xl ^ f)) for y in range(4) for xl in range(2)]
    return lax.ppermute(x, PLANE, pairs)


def flip(x, axis):
    return lax.ppermute(x, axis, [(0, 1), (1, 0)])


def dot(a, b, dims):
    return lax.dot_general(a, b, (dims, ((), ())), preferred_element_type=jnp.float32)


def pack_kernel(k, v, own):
    own[:TOK] = k[...]
    own[TOK:] = v[...]


def pack(keys, values):
    return pl.pallas_call(
        pack_kernel,
        grid=(1,),
        in_specs=[pl.BlockSpec(keys.shape, lambda i: (0, 0))] * 2,
        out_specs=pl.BlockSpec((2 * TOK, keys.shape[1]), lambda i: (0, 0)),
        out_shape=jax.ShapeDtypeStruct((2 * TOK, keys.shape[1]), jnp.bfloat16),
        compiler_params=pltpu.CompilerParams(vmem_limit_bytes=4 << 20),
        cost_estimate=pl.CostEstimate(
            flops=8 * keys.size, transcendentals=0, bytes_accessed=8 * keys.size
        ),
        name="pack",
    )(keys, values)


def attend_kernel(n_blocks, last, *refs):
    refs = list(refs)
    take = lambda n: [refs.pop(0) for _ in range(n)]
    q_refs, kv_refs = take(5), take(n_blocks)
    if last:
        far_k, far_v, o_in, ml_in = take(4)
        out_refs = take(8)
    else:
        o_out, ml_out = take(2)
    scale = LOG2E * DH**-0.5

    def operands(h):
        lanes = slice(h * DH, (h + 1) * DH)
        keys = [r[:TOK, lanes] for r in kv_refs]
        values = [r[TOK:, lanes] for r in kv_refs]
        if last:
            keys.append(far_k[:, lanes])
            values.append(far_v[:, lanes])
        return lanes, jnp.concatenate(keys, axis=0), jnp.concatenate(values, axis=0).T

    def scores(lanes, keys, j):
        pieces = q_refs[:3] if j == 0 else q_refs[3:]
        return dot(keys, jnp.concatenate([r[:, lanes] for r in pieces], axis=0), ((1,), (1,)))

    work = []
    for h in range(HEADS_LOCAL):
        lanes, keys, values = operands(h)
        for j in range(8 // SPAN):
            work.append((h, j, lanes, keys, values))
    lse = [[None] * (8 // SPAN) for _ in range(HEADS_LOCAL)]
    ahead = scores(*work[0][2:4], work[0][1])
    for i, (h, j, _, _, values) in enumerate(work):
        s = ahead
        if i + 1 < len(work):
            ahead = scores(*work[i + 1][2:4], work[i + 1][1])
        cols = slice(j * SPAN * TOK, (j + 1) * SPAN * TOK)
        rows = slice(h * DH, (h + 1) * DH)
        peak = jnp.max(s, axis=0, keepdims=True)
        if last:
            old_peak = ml_in[h, 0:1, cols]
            peak = jnp.maximum(peak, old_peak)
        p = jnp.exp2((s - peak) * scale)
        total = jnp.sum(p, axis=0, keepdims=True)
        summed = dot(values, p.astype(jnp.bfloat16), ((1,), (0,)))
        if last:
            decay = jnp.exp2((old_peak - peak) * scale)
            total = total + ml_in[h, 1:2, cols] * decay
            inverse = 1.0 / total
            summed = (summed * inverse + o_in[rows, cols] * (decay * inverse)).astype(jnp.bfloat16)
            for i in range(SPAN):
                out_refs[j * SPAN + i][rows, :] = summed[:, i * TOK : (i + 1) * TOK]
            lse[h][j] = peak * scale + jnp.log2(total)
        else:
            o_out[rows, cols] = summed
            ml_out[h, 0:1, cols] = peak
            ml_out[h, 1:2, cols] = total
    if last:
        whole = jnp.concatenate([jnp.concatenate(x, axis=1) for x in lse], axis=0)
        hi = whole.astype(jnp.bfloat16).astype(jnp.float32)
        mid = (whole - hi).astype(jnp.bfloat16).astype(jnp.float32)
        low = whole - hi - mid
        stats = jnp.concatenate([hi, mid, low, jnp.zeros_like(hi)], axis=0).astype(jnp.bfloat16)
        for r in range(8):
            out_refs[r][HEADS_LOCAL * DH :, :] = stats[:, r * TOK : (r + 1) * TOK]


def attend(queries, blocks, far, state):
    last = far is not None
    whole = lambda x: pl.BlockSpec(
        x.shape, lambda i: (0,) * len(x.shape), pipeline_mode=pl.Buffered(1)
    )
    operands = [*queries, *blocks] + ([*far, *state] if last else [])
    if last:
        out_shape = [
            jax.ShapeDtypeStruct((HEADS_LOCAL * DH + STAT_ROWS, TOK), jnp.bfloat16)
        ] * 8
    else:
        out_shape = [
            jax.ShapeDtypeStruct((HEADS_LOCAL * DH, 8 * TOK), jnp.float32),
            jax.ShapeDtypeStruct((HEADS_LOCAL, 2, 8 * TOK), jnp.float32),
        ]
    elements = HEADS_LOCAL * 8 * TOK * (len(blocks) + last) * TOK
    return pl.pallas_call(
        functools.partial(attend_kernel, len(blocks), last),
        grid=(1,),
        in_specs=[whole(x) for x in operands],
        out_specs=[whole(x) for x in out_shape],
        out_shape=out_shape,
        compiler_params=pltpu.CompilerParams(vmem_limit_bytes=VMEM),
        cost_estimate=pl.CostEstimate(
            flops=elements * DH * 12, transcendentals=elements, bytes_accessed=4 << 20
        ),
        name="attend",
    )(*operands)


def merge_kernel(*refs):
    parts, w_ref, sends, keeps = refs[:8], refs[8], refs[9:11], refs[11:13]
    att = refs[13]
    lse = []
    for r in range(8):
        s = parts[r][HEADS_LOCAL * DH :, :].astype(jnp.float32)
        lse.append(s[0:4] + s[4:8] + s[8:12])
    top = functools.reduce(jnp.maximum, lse)
    weights = [jnp.exp2(x - top) for x in lse]
    inverse = 1.0 / sum(weights)
    weights = [w * inverse for w in weights]
    c, xh = lax.axis_index("c"), lax.axis_index("xh")
    for h in range(HEADS_LOCAL):
        rows = slice(h * DH, (h + 1) * DH)
        merged = sum(parts[r][rows, :].astype(jnp.float32) * weights[r][h : h + 1, :] for r in range(8))
        tokens = merged.T.astype(jnp.bfloat16)
        for to in range(4):
            there = jnp.where(xh == to // 2, 2, 0) + jnp.where(c == to % 2, 1, 0)
            att[pl.ds(pl.multiple_of(there * 32, 32), 32), rows] = tokens[to * 32 : to * 32 + 32]
    for at in range(0, w_ref.shape[1], CHUNK):
        cols = slice(at, at + CHUNK)
        product = dot(att[...], w_ref[:, cols], ((1,), (0,)))
        for side in range(2):
            sends[side][:, cols] = product[side * 64 : side * 64 + 32].astype(jnp.bfloat16)
            keeps[side][:, cols] = product[side * 64 + 32 : side * 64 + 64]


def project(parts, weight):
    depth, width = weight.shape
    whole = lambda x: pl.BlockSpec(x.shape, lambda i: (0,) * len(x.shape))
    out_shape = [
        jax.ShapeDtypeStruct((32, width), dtype)
        for dtype in (jnp.bfloat16, jnp.bfloat16, jnp.float32, jnp.float32)
    ]
    return pl.pallas_call(
        merge_kernel,
        grid=(1,),
        in_specs=[whole(x) for x in parts]
            + [
                pl.BlockSpec(
                    weight.shape, lambda i: (0, 0), pipeline_mode=pl.Buffered(1)
                )
            ],
        out_specs=[whole(x) for x in out_shape],
        scratch_shapes=[pltpu.VMEM((TOK, depth), jnp.bfloat16)],
        out_shape=out_shape,
        compiler_params=pltpu.CompilerParams(vmem_limit_bytes=VMEM),
        cost_estimate=pl.CostEstimate(
            flops=2 * TOK * depth * width, transcendentals=4096, bytes_accessed=6 << 20
        ),
        name="merge_project",
    )(*parts, weight)


def body(queries, key_vectors, value_vectors, out_weight):
    own = pack(key_vectors, value_vectors)
    pair = pack(queries, flip(queries, "xl"))
    up, down = shift(own, "z", 1), shift(own, "z", -1)
    blocks = [own, up, down]
    up, down, pair = lax.optimization_barrier((up, down, pair))
    above, below = shift(pair, "y", 1), shift(pair, "y", -1)
    up, down = shift(up, "z", 1), shift(down, "z", -1)
    blocks += [up, down]
    up, down, above, below = lax.optimization_barrier((up, down, above, below))
    up, down = shift(up, "z", 1), shift(down, "z", -1)
    blocks += [up, down]
    far = (shift(up[:TOK], "z", 1), shift(down[TOK:], "z", -1))
    q_parts = [pair, shift(above[:TOK], "y", 1), shift(below[TOK:], "y", -1), above, below]
    state = attend(q_parts, blocks, None, None)
    parts = attend(q_parts, [], far, state)
    parts = list(parts)
    for r in FIRST_OUT:
        parts[r] = to_slot(parts[r], SLOTS[r])
    send_other, send_own, keep_other, keep_own = project(parts, out_weight)
    other = keep_other + flip(send_other, "c").astype(jnp.float32)
    arrived = flip(other.astype(jnp.bfloat16), "xh").astype(jnp.float32)
    return keep_own + flip(send_own, "c").astype(jnp.float32) + arrived


def solution(mesh):
    fine = Mesh(mesh.devices.reshape(tuple(AXES.values())), tuple(AXES))
    ctx, head = ("z", "y", "xl"), ("xh", "c")
    placed = (P(ctx, head), P(ctx, head), P(ctx, head), P(head, None))
    return jax.shard_map(
        body, mesh=fine, in_specs=placed, out_specs=P(ctx + head, None), check_vma=False
    )
```

```python
import functools

import jax
import jax.numpy as jnp
from jax import lax
from jax.experimental import pallas as pl
from jax.experimental.pallas import tpu as pltpu
from jax.sharding import Mesh, PartitionSpec as P

DH = 128
AXES = {"z": 8, "y": 4, "xl": 2, "xh": 2, "c": 2}
PLANE = ("y", "xl")
SLOTS = ((0, 0), (0, 1), (2, 0), (2, 1), (-1, 0), (-1, 1), (1, 0), (1, 1))
FIRST_OUT = (2, 3, 5, 7, 4, 6, 1)
SPAN = 4
LOG2E = 1.4426950408889634
TOK = 128
HEADS_LOCAL = 4
STAT_ROWS = 16
VMEM = 13 * 1024 * 1024
CHUNK = 1024


def shift(x, axis, by):
    n = AXES[axis]
    return lax.ppermute(x, axis, [(i, (i + by) % n) for i in range(n)])


def to_slot(x, slot):
    dy, f = slot
    pairs = [(y * 2 + xl, (y + dy) % 4 * 2 + (xl ^ f)) for y in range(4) for xl in range(2)]
    return lax.ppermute(x, PLANE, pairs)


def flip(x, axis):
    return lax.ppermute(x, axis, [(0, 1), (1, 0)])


def dot(a, b, dims):
    return lax.dot_general(a, b, (dims, ((), ())), preferred_element_type=jnp.float32)


def pack_kernel(k, v, own):
    own[:TOK] = k[...]
    own[TOK:] = v[...]


def pack(keys, values):
    return pl.pallas_call(
        pack_kernel,
        grid=(1,),
        in_specs=[pl.BlockSpec(keys.shape, lambda i: (0, 0))] * 2,
        out_specs=pl.BlockSpec((2 * TOK, keys.shape[1]), lambda i: (0, 0)),
        out_shape=jax.ShapeDtypeStruct((2 * TOK, keys.shape[1]), jnp.bfloat16),
        compiler_params=pltpu.CompilerParams(vmem_limit_bytes=4 << 20),
        cost_estimate=pl.CostEstimate(
            flops=8 * keys.size, transcendentals=0, bytes_accessed=8 * keys.size
        ),
        name="pack",
    )(keys, values)


def attend_kernel(n_blocks, last, *refs):
    refs = list(refs)
    take = lambda n: [refs.pop(0) for _ in range(n)]
    q_refs, kv_refs = take(5), take(n_blocks)
    if last:
        far_k, far_v, o_in, ml_in = take(4)
        out_refs = take(8)
    else:
        o_out, ml_out = take(2)
    scale = LOG2E * DH**-0.5

    def operands(h):
        lanes = slice(h * DH, (h + 1) * DH)
        keys = [r[:TOK, lanes] for r in kv_refs]
        values = [r[TOK:, lanes] for r in kv_refs]
        if last:
            keys.append(far_k[:, lanes])
            values.append(far_v[:, lanes])
        return lanes, jnp.concatenate(keys, axis=0), jnp.concatenate(values, axis=0).T

    def scores(lanes, keys, j):
        pieces = q_refs[:3] if j == 0 else q_refs[3:]
        return dot(keys, jnp.concatenate([r[:, lanes] for r in pieces], axis=0), ((1,), (1,)))

    work = []
    for h in range(HEADS_LOCAL):
        lanes, keys, values = operands(h)
        for j in range(8 // SPAN):
            work.append((h, j, lanes, keys, values))
    lse = [[None] * (8 // SPAN) for _ in range(HEADS_LOCAL)]
    ahead = scores(*work[0][2:4], work[0][1])
    for i, (h, j, _, _, values) in enumerate(work):
        s = ahead
        if i + 1 < len(work):
            ahead = scores(*work[i + 1][2:4], work[i + 1][1])
        cols = slice(j * SPAN * TOK, (j + 1) * SPAN * TOK)
        rows = slice(h * DH, (h + 1) * DH)
        peak = jnp.max(s, axis=0, keepdims=True)
        if last:
            old_peak = ml_in[h, 0:1, cols]
            peak = jnp.maximum(peak, old_peak)
        p = jnp.exp2((s - peak) * scale)
        total = jnp.sum(p, axis=0, keepdims=True)
        summed = dot(values, p.astype(jnp.bfloat16), ((1,), (0,)))
        if last:
            decay = jnp.exp2((old_peak - peak) * scale)
            total = total + ml_in[h, 1:2, cols] * decay
            inverse = 1.0 / total
            summed = (summed * inverse + o_in[rows, cols] * (decay * inverse)).astype(jnp.bfloat16)
            for i in range(SPAN):
                out_refs[j * SPAN + i][rows, :] = summed[:, i * TOK : (i + 1) * TOK]
            lse[h][j] = peak * scale + jnp.log2(total)
        else:
            o_out[rows, cols] = summed
            ml_out[h, 0:1, cols] = peak
            ml_out[h, 1:2, cols] = total
    if last:
        whole = jnp.concatenate([jnp.concatenate(x, axis=1) for x in lse], axis=0)
        hi = whole.astype(jnp.bfloat16).astype(jnp.float32)
        mid = (whole - hi).astype(jnp.bfloat16).astype(jnp.float32)
        low = whole - hi - mid
        stats = jnp.concatenate([hi, mid, low, jnp.zeros_like(hi)], axis=0).astype(jnp.bfloat16)
        for r in range(8):
            out_refs[r][HEADS_LOCAL * DH :, :] = stats[:, r * TOK : (r + 1) * TOK]


def attend(queries, blocks, far, state):
    last = far is not None
    whole = lambda x: pl.BlockSpec(
        x.shape, lambda i: (0,) * len(x.shape), pipeline_mode=pl.Buffered(1)
    )
    operands = [*queries, *blocks] + ([*far, *state] if last else [])
    if last:
        out_shape = [
            jax.ShapeDtypeStruct((HEADS_LOCAL * DH + STAT_ROWS, TOK), jnp.bfloat16)
        ] * 8
    else:
        out_shape = [
            jax.ShapeDtypeStruct((HEADS_LOCAL * DH, 8 * TOK), jnp.float32),
            jax.ShapeDtypeStruct((HEADS_LOCAL, 2, 8 * TOK), jnp.float32),
        ]
    elements = HEADS_LOCAL * 8 * TOK * (len(blocks) + last) * TOK
    return pl.pallas_call(
        functools.partial(attend_kernel, len(blocks), last),
        grid=(1,),
        in_specs=[whole(x) for x in operands],
        out_specs=[whole(x) for x in out_shape],
        out_shape=out_shape,
        compiler_params=pltpu.CompilerParams(vmem_limit_bytes=VMEM),
        cost_estimate=pl.CostEstimate(
            flops=elements * DH * 12, transcendentals=elements, bytes_accessed=4 << 20
        ),
        name="attend",
    )(*operands)


def merge_kernel(*refs):
    parts, w_ref, sends, keeps = refs[:8], refs[8], refs[9:11], refs[11:13]
    att = refs[13]
    lse = []
    for r in range(8):
        s = parts[r][HEADS_LOCAL * DH :, :].astype(jnp.float32)
        lse.append(s[0:4] + s[4:8] + s[8:12])
    top = functools.reduce(jnp.maximum, lse)
    weights = [jnp.exp2(x - top) for x in lse]
    inverse = 1.0 / sum(weights)
    weights = [w * inverse for w in weights]
    c, xh = lax.axis_index("c"), lax.axis_index("xh")
    for h in range(HEADS_LOCAL):
        rows = slice(h * DH, (h + 1) * DH)
        merged = sum(parts[r][rows, :].astype(jnp.float32) * weights[r][h : h + 1, :] for r in range(8))
        tokens = merged.T.astype(jnp.bfloat16)
        for to in range(4):
            there = jnp.where(xh == to // 2, 2, 0) + jnp.where(c == to % 2, 1, 0)
            att[pl.ds(pl.multiple_of(there * 32, 32), 32), rows] = tokens[to * 32 : to * 32 + 32]
    for at in range(0, w_ref.shape[1], CHUNK):
        cols = slice(at, at + CHUNK)
        product = dot(att[...], w_ref[:, cols], ((1,), (0,)))
        for side in range(2):
            sends[side][:, cols] = product[side * 64 : side * 64 + 32].astype(jnp.bfloat16)
            keeps[side][:, cols] = product[side * 64 + 32 : side * 64 + 64]


def project(parts, weight):
    depth, width = weight.shape
    whole = lambda x: pl.BlockSpec(x.shape, lambda i: (0,) * len(x.shape))
    out_shape = [
        jax.ShapeDtypeStruct((32, width), dtype)
        for dtype in (jnp.bfloat16, jnp.bfloat16, jnp.float32, jnp.float32)
    ]
    return pl.pallas_call(
        merge_kernel,
        grid=(1,),
        in_specs=[whole(x) for x in parts]
            + [
                pl.BlockSpec(
                    weight.shape, lambda i: (0, 0), pipeline_mode=pl.Buffered(1)
                )
            ],
        out_specs=[whole(x) for x in out_shape],
        scratch_shapes=[pltpu.VMEM((TOK, depth), jnp.bfloat16)],
        out_shape=out_shape,
        compiler_params=pltpu.CompilerParams(vmem_limit_bytes=VMEM),
        cost_estimate=pl.CostEstimate(
            flops=2 * TOK * depth * width, transcendentals=4096, bytes_accessed=6 << 20
        ),
        name="merge_project",
    )(*parts, weight)


def body(queries, key_vectors, value_vectors, out_weight):
    own = pack(key_vectors, value_vectors)
    pair = pack(queries, flip(queries, "xl"))
    up, down = shift(own, "z", 1), shift(own, "z", -1)
    blocks = [own, up, down]
    up, down, pair = lax.optimization_barrier((up, down, pair))
    above, below = shift(pair, "y", 1), shift(pair, "y", -1)
    up, down = shift(up, "z", 1), shift(down, "z", -1)
    blocks += [up, down]
    up, down = shift(up, "z", 1), shift(down, "z", -1)
    blocks += [up, down]
    far = (shift(up[:TOK], "z", 1), shift(down[TOK:], "z", -1))
    q_parts = [pair, shift(above[:TOK], "y", 1), shift(below[TOK:], "y", -1), above, below]
    state = attend(q_parts, blocks, None, None)
    parts = attend(q_parts, [], far, state)
    parts = list(parts)
    for r in FIRST_OUT:
        parts[r] = to_slot(parts[r], SLOTS[r])
    send_other, send_own, keep_other, keep_own = project([parts[r] for r in FIRST_OUT] + parts[:1], out_weight)
    other = keep_other + flip(send_other, "c").astype(jnp.float32)
    arrived = flip(other.astype(jnp.bfloat16), "xh").astype(jnp.float32)
    return keep_own + flip(send_own, "c").astype(jnp.float32) + arrived


def solution(mesh):
    fine = Mesh(mesh.devices.reshape(tuple(AXES.values())), tuple(AXES))
    ctx, head = ("z", "y", "xl"), ("xh", "c")
    placed = (P(ctx, head), P(ctx, head), P(ctx, head), P(head, None))
    return jax.shard_map(
        body, mesh=fine, in_specs=placed, out_specs=P(ctx + head, None), check_vma=False
    )
```

```python
import functools

import jax
import jax.numpy as jnp
from jax import lax
from jax.experimental import pallas as pl
from jax.experimental.pallas import tpu as pltpu
from jax.sharding import Mesh, PartitionSpec as P

DH = 128
AXES = {"z": 8, "y": 4, "xl": 2, "xh": 2, "c": 2}
PLANE = ("y", "xl")
SLOTS = ((0, 0), (0, 1), (2, 0), (2, 1), (-1, 0), (-1, 1), (1, 0), (1, 1))
FIRST_OUT = (5, 7, 3, 2, 4, 6, 1)
SPAN = 4
LOG2E = 1.4426950408889634
TOK = 128
HEADS_LOCAL = 4
STAT_ROWS = 16
VMEM = 13 * 1024 * 1024
CHUNK = 1024


def shift(x, axis, by):
    n = AXES[axis]
    return lax.ppermute(x, axis, [(i, (i + by) % n) for i in range(n)])


def to_slot(x, slot):
    dy, f = slot
    pairs = [(y * 2 + xl, (y + dy) % 4 * 2 + (xl ^ f)) for y in range(4) for xl in range(2)]
    return lax.ppermute(x, PLANE, pairs)


def flip(x, axis):
    return lax.ppermute(x, axis, [(0, 1), (1, 0)])


def dot(a, b, dims):
    return lax.dot_general(a, b, (dims, ((), ())), preferred_element_type=jnp.float32)


def pack_kernel(k, v, own):
    own[:TOK] = k[...]
    own[TOK:] = v[...]


def pack(keys, values):
    return pl.pallas_call(
        pack_kernel,
        grid=(1,),
        in_specs=[pl.BlockSpec(keys.shape, lambda i: (0, 0))] * 2,
        out_specs=pl.BlockSpec((2 * TOK, keys.shape[1]), lambda i: (0, 0)),
        out_shape=jax.ShapeDtypeStruct((2 * TOK, keys.shape[1]), jnp.bfloat16),
        compiler_params=pltpu.CompilerParams(vmem_limit_bytes=4 << 20),
        cost_estimate=pl.CostEstimate(
            flops=8 * keys.size, transcendentals=0, bytes_accessed=8 * keys.size
        ),
        name="pack",
    )(keys, values)


def attend_kernel(n_blocks, last, *refs):
    refs = list(refs)
    take = lambda n: [refs.pop(0) for _ in range(n)]
    q_refs, kv_refs = take(5), take(n_blocks)
    if last:
        far_k, far_v, o_in, ml_in = take(4)
        out_refs = take(8)
    else:
        o_out, ml_out = take(2)
    scale = LOG2E * DH**-0.5

    def operands(h):
        lanes = slice(h * DH, (h + 1) * DH)
        keys = [r[:TOK, lanes] for r in kv_refs]
        values = [r[TOK:, lanes] for r in kv_refs]
        if last:
            keys.append(far_k[:, lanes])
            values.append(far_v[:, lanes])
        return lanes, jnp.concatenate(keys, axis=0), jnp.concatenate(values, axis=0).T

    def scores(lanes, keys, j):
        pieces = q_refs[:3] if j == 0 else q_refs[3:]
        return dot(keys, jnp.concatenate([r[:, lanes] for r in pieces], axis=0), ((1,), (1,)))

    work = []
    for h in range(HEADS_LOCAL):
        lanes, keys, values = operands(h)
        for j in range(8 // SPAN):
            work.append((h, j, lanes, keys, values))
    lse = [[None] * (8 // SPAN) for _ in range(HEADS_LOCAL)]
    ahead = scores(*work[0][2:4], work[0][1])
    for i, (h, j, _, _, values) in enumerate(work):
        s = ahead
        if i + 1 < len(work):
            ahead = scores(*work[i + 1][2:4], work[i + 1][1])
        cols = slice(j * SPAN * TOK, (j + 1) * SPAN * TOK)
        rows = slice(h * DH, (h + 1) * DH)
        peak = jnp.max(s, axis=0, keepdims=True)
        if last:
            old_peak = ml_in[h, 0:1, cols]
            peak = jnp.maximum(peak, old_peak)
        p = jnp.exp2((s - peak) * scale)
        total = jnp.sum(p, axis=0, keepdims=True)
        summed = dot(values, p.astype(jnp.bfloat16), ((1,), (0,)))
        if last:
            decay = jnp.exp2((old_peak - peak) * scale)
            total = total + ml_in[h, 1:2, cols] * decay
            inverse = 1.0 / total
            summed = (summed * inverse + o_in[rows, cols] * (decay * inverse)).astype(jnp.bfloat16)
            for i in range(SPAN):
                out_refs[j * SPAN + i][rows, :] = summed[:, i * TOK : (i + 1) * TOK]
            lse[h][j] = peak * scale + jnp.log2(total)
        else:
            o_out[rows, cols] = summed
            ml_out[h, 0:1, cols] = peak
            ml_out[h, 1:2, cols] = total
    if last:
        whole = jnp.concatenate([jnp.concatenate(x, axis=1) for x in lse], axis=0)
        hi = whole.astype(jnp.bfloat16).astype(jnp.float32)
        mid = (whole - hi).astype(jnp.bfloat16).astype(jnp.float32)
        low = whole - hi - mid
        stats = jnp.concatenate([hi, mid, low, jnp.zeros_like(hi)], axis=0).astype(jnp.bfloat16)
        for r in range(8):
            out_refs[r][HEADS_LOCAL * DH :, :] = stats[:, r * TOK : (r + 1) * TOK]


def attend(queries, blocks, far, state):
    last = far is not None
    whole = lambda x: pl.BlockSpec(
        x.shape, lambda i: (0,) * len(x.shape), pipeline_mode=pl.Buffered(1)
    )
    operands = [*queries, *blocks] + ([*far, *state] if last else [])
    if last:
        out_shape = [
            jax.ShapeDtypeStruct((HEADS_LOCAL * DH + STAT_ROWS, TOK), jnp.bfloat16)
        ] * 8
    else:
        out_shape = [
            jax.ShapeDtypeStruct((HEADS_LOCAL * DH, 8 * TOK), jnp.float32),
            jax.ShapeDtypeStruct((HEADS_LOCAL, 2, 8 * TOK), jnp.float32),
        ]
    elements = HEADS_LOCAL * 8 * TOK * (len(blocks) + last) * TOK
    return pl.pallas_call(
        functools.partial(attend_kernel, len(blocks), last),
        grid=(1,),
        in_specs=[whole(x) for x in operands],
        out_specs=[whole(x) for x in out_shape],
        out_shape=out_shape,
        compiler_params=pltpu.CompilerParams(vmem_limit_bytes=VMEM),
        cost_estimate=pl.CostEstimate(
            flops=elements * DH * 12, transcendentals=elements, bytes_accessed=4 << 20
        ),
        name="attend",
    )(*operands)


def merge_kernel(*refs):
    parts, w_ref, sends, keeps = refs[:8], refs[8], refs[9:11], refs[11:13]
    att = refs[13]
    lse = []
    for r in range(8):
        s = parts[r][HEADS_LOCAL * DH :, :].astype(jnp.float32)
        lse.append(s[0:4] + s[4:8] + s[8:12])
    top = functools.reduce(jnp.maximum, lse)
    weights = [jnp.exp2(x - top) for x in lse]
    inverse = 1.0 / sum(weights)
    weights = [w * inverse for w in weights]
    c, xh = lax.axis_index("c"), lax.axis_index("xh")
    for h in range(HEADS_LOCAL):
        rows = slice(h * DH, (h + 1) * DH)
        merged = sum(parts[r][rows, :].astype(jnp.float32) * weights[r][h : h + 1, :] for r in range(8))
        tokens = merged.T.astype(jnp.bfloat16)
        for to in range(4):
            there = jnp.where(xh == to // 2, 2, 0) + jnp.where(c == to % 2, 1, 0)
            att[pl.ds(pl.multiple_of(there * 32, 32), 32), rows] = tokens[to * 32 : to * 32 + 32]
    for at in range(0, w_ref.shape[1], CHUNK):
        cols = slice(at, at + CHUNK)
        product = dot(att[...], w_ref[:, cols], ((1,), (0,)))
        for side in range(2):
            sends[side][:, cols] = product[side * 64 : side * 64 + 32].astype(jnp.bfloat16)
            keeps[side][:, cols] = product[side * 64 + 32 : side * 64 + 64]


def project(parts, weight):
    depth, width = weight.shape
    whole = lambda x: pl.BlockSpec(x.shape, lambda i: (0,) * len(x.shape))
    out_shape = [
        jax.ShapeDtypeStruct((32, width), dtype)
        for dtype in (jnp.bfloat16, jnp.bfloat16, jnp.float32, jnp.float32)
    ]
    return pl.pallas_call(
        merge_kernel,
        grid=(1,),
        in_specs=[whole(x) for x in parts]
            + [
                pl.BlockSpec(
                    weight.shape, lambda i: (0, 0), pipeline_mode=pl.Buffered(1)
                )
            ],
        out_specs=[whole(x) for x in out_shape],
        scratch_shapes=[pltpu.VMEM((TOK, depth), jnp.bfloat16)],
        out_shape=out_shape,
        compiler_params=pltpu.CompilerParams(vmem_limit_bytes=VMEM),
        cost_estimate=pl.CostEstimate(
            flops=2 * TOK * depth * width, transcendentals=4096, bytes_accessed=6 << 20
        ),
        name="merge_project",
    )(*parts, weight)


def body(queries, key_vectors, value_vectors, out_weight):
    own = pack(key_vectors, value_vectors)
    pair = pack(queries, flip(queries, "xl"))
    up, down = shift(own, "z", 1), shift(own, "z", -1)
    blocks = [own, up, down]
    up, down, pair = lax.optimization_barrier((up, down, pair))
    above, below = shift(pair, "y", 1), shift(pair, "y", -1)
    up, down = shift(up, "z", 1), shift(down, "z", -1)
    blocks += [up, down]
    up, down = shift(up, "z", 1), shift(down, "z", -1)
    blocks += [up, down]
    far = (shift(up[:TOK], "z", 1), shift(down[TOK:], "z", -1))
    q_parts = [pair, shift(above[:TOK], "y", 1), shift(below[TOK:], "y", -1), above, below]
    state = attend(q_parts, blocks, None, None)
    parts = attend(q_parts, [], far, state)
    parts = list(parts)
    for r in FIRST_OUT:
        parts[r] = to_slot(parts[r], SLOTS[r])
    send_other, send_own, keep_other, keep_own = project([parts[r] for r in FIRST_OUT] + parts[:1], out_weight)
    other = keep_other + flip(send_other, "c").astype(jnp.float32)
    arrived = flip(other.astype(jnp.bfloat16), "xh").astype(jnp.float32)
    return keep_own + flip(send_own, "c").astype(jnp.float32) + arrived


def solution(mesh):
    fine = Mesh(mesh.devices.reshape(tuple(AXES.values())), tuple(AXES))
    ctx, head = ("z", "y", "xl"), ("xh", "c")
    placed = (P(ctx, head), P(ctx, head), P(ctx, head), P(head, None))
    return jax.shard_map(
        body, mesh=fine, in_specs=placed, out_specs=P(ctx + head, None), check_vma=False
    )
```
